512 devices in a mesh: seq: 64 (over x, z, core), head: 8 (over y).
Axes of the slice: x: 4, y: 8, z: 8, core: 2. Of those that a mesh axis runs over, the one named last changes fastest.
Arguments:
- queries: bfloat16 [32768, 2048], P(('seq', 'head')), may hold values from -6 to 6
- keys: bfloat16 [32768, 512], P(('seq', 'head')), may hold values from -6 to 6
- values: bfloat16 [32768, 512], P(('seq', 'head')), may hold values from -6 to 6
- vertical: int32 [16, 64], replicated, may hold values from 0 to 511, as said below
- offsets: int32 [16, 5], replicated, may hold values from 0 to 7, as said below
Outputs:
- attended: bfloat16 [32768, 2048], P(('seq', 'head'))
The draws below stay inside these ranges and needn't reach their ends.
Inputs may be any that keep to these rules, and one draw needn't show every extreme that they name: `vertical`: entry [h, s + i], for i below 1, is a block of segment s, from s * 8 to (s + 1) * 8 - 1; the blocks of one head in one segment are distinct. The 5 offsets of one head are distinct and include 0 and 7.
All inputs are finite; a program needn't handle non-finite values.
Results may differ from the reference program's by a relative error of at most 0.0032.
Values may be sent and summed in bfloat16 or wider, within the bound.
A program may use at most 64 MiB of HBM per device.

```python
import jax
import jax.numpy as jnp
from jax import lax

HEADS = 16
KV_HEADS = 4
HDIM = 128
BLOCK = 64
NS = 5
VPS = 1
SEG_BLOCKS = 8
TOKENS = 32768
NV = 64


def draw_queries(key, part):
    key = jax.random.fold_in(key, 1)
    base = jnp.clip(jax.random.normal(key, (TOKENS, HEADS * HDIM), jnp.float32), -6.0, 6.0)
    return base.astype(jnp.bfloat16)


def draw_keys(key, part):
    key = jax.random.fold_in(key, 2)
    base = jnp.clip(2.5 * jax.random.normal(key, (TOKENS, KV_HEADS * HDIM), jnp.float32), -6.0, 6.0)
    return base.astype(jnp.bfloat16)


def draw_vertical(key, part):
    key = jax.random.fold_in(key, 3)
    segments = NV // VPS
    ranks = jax.random.randint(key, (HEADS, segments, SEG_BLOCKS), 0, 1 << 20) * SEG_BLOCKS
    ranks = ranks + jnp.arange(SEG_BLOCKS)[None, None, :]
    ranks = ranks.at[0, 0, 0].set(-1)
    ranks = ranks.at[0, segments - 1, SEG_BLOCKS - 1].set(-1)
    selected_entries = jnp.argsort(ranks, axis=-1)[..., :VPS]
    starts = jnp.arange(segments)[None, :, None] * SEG_BLOCKS
    return (selected_entries + starts).reshape(HEADS, NV).astype(jnp.int32)


def draw_offsets(key, part):
    key = jax.random.fold_in(key, 4)
    inner = SEG_BLOCKS - 2
    ranks = jax.random.randint(key, (HEADS, inner), 0, 1 << 20) * inner + jnp.arange(inner)[None, :]
    selected_entries = jnp.argsort(ranks, axis=-1)[:, :NS - 2] + 1
    ends = jnp.broadcast_to(jnp.array([0, SEG_BLOCKS - 1]), (HEADS, 2))
    return jnp.concatenate([ends, selected_entries], axis=1).astype(jnp.int32)


def level_of(stream_key, dims, pieces, least, top_value):
    level, own = 1.0, jax.random.fold_in(stream_key, 6)
    for dim, shards_of in pieces:
        steps = jnp.exp(jax.random.uniform(jax.random.fold_in(own, dim), (shards_of,), jnp.float32, least / len(pieces), top_value / len(pieces)))
        level = level * jnp.repeat(steps, dims[dim] // shards_of).reshape([-1 if axis == dim else 1 for axis in range(len(dims))])
    return level


def scatter_about(rng, extent, deviation, most, cuts=(), kind=jnp.bfloat16):
    values = jax.random.normal(rng, extent, jnp.float32) * deviation
    if len(cuts) > 0:
        values = level_of(rng, extent, cuts, -0.22, 0.18) * values
    return jnp.clip(values, min=-most, max=most).astype(kind)


def setup_inputs(seed: int = 0) -> dict:
    key_of = jax.random.split(jax.random.key(seed), 6)
    return {
        "queries": draw_queries(jax.random.fold_in(key_of[5], 71), 0),
        "keys": draw_keys(jax.random.fold_in(key_of[5], 71), 0),
        "values": scatter_about(key_of[2], (TOKENS, KV_HEADS * HDIM), 1.0, 6.0, ((0, 512),)),
        "vertical": draw_vertical(jax.random.fold_in(key_of[5], 71), 0),
        "offsets": draw_offsets(jax.random.fold_in(key_of[5], 71), 0),
    }


def reference(queries, keys, values, vertical, offsets):
    blocks_total = TOKENS // BLOCK
    group = HEADS // KV_HEADS
    scale = HDIM ** -0.5
    query_blocks = queries.reshape(blocks_total, BLOCK, HEADS, HDIM)
    key_blocks = keys.reshape(blocks_total, BLOCK, KV_HEADS, HDIM)
    value_blocks = values.reshape(blocks_total, BLOCK, KV_HEADS, HDIM)
    position = jnp.arange(BLOCK).astype(jnp.int32)
    causal = position[None, :] <= position[:, None]

    def one_head(head):
        kv_index = head // group
        head_queries = lax.dynamic_index_in_dim(query_blocks, head, 2, keepdims=False)
        head_keys = lax.dynamic_index_in_dim(key_blocks, kv_index, 2, keepdims=False)
        head_values = lax.dynamic_index_in_dim(value_blocks, kv_index, 2, keepdims=False)
        vert_ids = lax.dynamic_index_in_dim(vertical, head, 0, keepdims=False).astype(jnp.int32)
        slash_ids = lax.dynamic_index_in_dim(offsets, head, 0, keepdims=False).astype(jnp.int32)
        vert_keys = jnp.take(head_keys, vert_ids, axis=0).astype(jnp.float32)
        vert_values = jnp.take(head_values, vert_ids, axis=0).astype(jnp.float32)

        def one_block(block):
            query_rows = lax.dynamic_index_in_dim(head_queries, block, 0, keepdims=False).astype(jnp.float32)
            distance = block - vert_ids
            on_slash = jnp.any(distance[:, None] == slash_ids[None, :], axis=1)
            vert_keep = (distance > 0) & jnp.logical_not(on_slash)
            vert_scores = jnp.einsum('qd,nkd->qnk', query_rows, vert_keys) * scale
            vert_scores = jnp.where(vert_keep[None, :, None], vert_scores, -jnp.inf)
            source = block - slash_ids
            slash_keep = source >= 0
            source = jnp.maximum(source, 0).astype(jnp.int32)
            slant_band_indices = jnp.take(head_keys, source, axis=0).astype(jnp.float32)
            diagonal_values = jnp.take(head_values, source, axis=0).astype(jnp.float32)
            slash_scores = jnp.einsum('qd,nkd->qnk', query_rows, slant_band_indices) * scale
            allowed = slash_keep[None, :, None] & ((slash_ids[None, :, None] != 0) | causal[:, None, :])
            slash_scores = jnp.where(allowed, slash_scores, -jnp.inf)
            top = jnp.maximum(jnp.max(vert_scores, axis=(1, 2)), jnp.max(slash_scores, axis=(1, 2)))
            vert_weights = jnp.exp(vert_scores - top[:, None, None])
            slash_weights = jnp.exp(slash_scores - top[:, None, None])
            total = jnp.sum(vert_weights, axis=(1, 2)) + jnp.sum(slash_weights, axis=(1, 2))
            vert_round = lax.optimization_barrier(vert_weights.astype(jnp.bfloat16)).astype(jnp.float32)
            diagonal_rounded = lax.optimization_barrier(slash_weights.astype(jnp.bfloat16)).astype(jnp.float32)
            output = jnp.einsum('qnk,nkd->qd', vert_round, vert_values)
            output = output + jnp.einsum('qnk,nkd->qd', diagonal_rounded, diagonal_values)
            return (output / total[:, None]).astype(jnp.bfloat16)

        return lax.map(one_block, jnp.arange(blocks_total).astype(jnp.int32))

    result = lax.map(one_head, jnp.arange(HEADS).astype(jnp.int32))
    return jnp.transpose(result, (1, 2, 0, 3)).reshape(TOKENS, HEADS * HDIM)
```

```python
import functools
import math

import jax
import jax.numpy as jnp
from jax import lax
from jax.experimental import pallas as pl
from jax.experimental.pallas import tpu as pltpu
from jax.sharding import PartitionSpec as P

HDIM = 128
BLOCK = 64
NX, NZ, NC = 4, 8, 2
LOW = -1e30
RATE = HDIM ** (-0.5) * math.log2(math.e)
MESH = pl.DeviceIdType.MESH


def kernel(
    ny,
    ns,
    q_ref,
    k_ref,
    v_ref,
    vert_ref,
    offs_ref,
    out_ref,
    qbuf,
    own_k,
    own_v,
    raw,
    prior,
    vert,
    bias_l,
    score_l,
    score_a,
    score_b,
    peak,
    sums,
    acc,
    obuf,
    y_send,
    y_recv,
    ring_send,
    ring_recv,
    bx_send,
    bx_recv,
    az_send,
    az_recv,
    sib_send,
    sib_recv,
    misc,
    out_send,
    out_recv,
):
    s = lax.axis_index("seq")
    j = lax.axis_index("head")
    core = lax.rem(s, NC)
    z = lax.rem(s // NC, NZ)
    x = s // (NC * NZ)
    nseq = NX * NZ * NC
    rows = ny * BLOCK
    own = (own_k, own_v)

    def at(px, pz, pc):
        return (lax.rem(px + NX, NX) * NZ + lax.rem(pz + NZ, NZ)) * NC + pc

    up_z, dn_z = at(x, z + 1, core), at(x, z - 1, core)
    up_x, dn_x = at(x + 1, z, core), at(x - 1, z, core)
    sib = at(x, z, 1 - core)
    after = lax.rem(s + 1, nseq)
    before = lax.rem(s + nseq - 1, nseq)
    across_x = [at(x + r, z, core) for r in range(1, NX)]
    reach = NZ // 2 - 1
    along_z = {d: at(x, z + d, core) for r in range(1, reach + 1) for d in (r, -r)}
    far_z = {d: other for d, other in along_z.items() if abs(d) > 1}

    kv_col = pl.multiple_of((j // 2) * HDIM, HDIM)
    q_col = pl.multiple_of(j * 2 * HDIM, 2 * HDIM)
    here = [
        pltpu.make_async_copy(k_ref.at[:, pl.ds(kv_col, HDIM)], own_k.at[j], misc.at[0]),
        pltpu.make_async_copy(v_ref.at[:, pl.ds(kv_col, HDIM)], own_v.at[j], misc.at[1]),
        pltpu.make_async_copy(q_ref.at[:, pl.ds(q_col, 2 * HDIM)], qbuf.at[j], misc.at[2]),
    ]
    for copy in here:
        copy.start()

    barrier = pltpu.get_barrier_semaphore()
    for r in range(1, ny):
        pl.semaphore_signal(
            barrier, inc=1, device_id=(s, lax.rem(j + r, ny)), device_id_type=MESH
        )
    others = [up_z, dn_z, sib, after, before] + across_x + list(far_z.values())
    for other in others:
        pl.semaphore_signal(barrier, inc=1, device_id=(other, j), device_id_type=MESH)
    pl.semaphore_wait(barrier, ny - 1 + len(others))

    sent = []

    def remote(src, dst, device, send_sem, recv_sem):
        copy = pltpu.make_async_remote_copy(
            src, dst, send_sem, recv_sem, device_id=device, device_id_type=MESH
        )
        copy.start()
        sent.append(copy)

    def send(src, to, send_sem, recv_sem):
        remote(src, src, (to, j), send_sem, recv_sem)

    def arrived(dst, sem):
        pltpu.make_async_copy(dst, dst, sem).wait()

    order = sorted(range(1, ny), key=lambda r: -min(r, ny - r))

    def y_start(kind):
        for r in order:
            to = lax.rem(j + r, ny)
            if kind == 3:
                col = pl.multiple_of((to // 2) * HDIM, HDIM)
                src, dst = raw.at[:, :, pl.ds(col, HDIM)], prior.at[:, j]
            elif kind == 2:
                col = pl.multiple_of(to * 2 * HDIM, 2 * HDIM)
                src, dst = q_ref.at[:, pl.ds(col, 2 * HDIM)], qbuf.at[j]
            else:
                col = pl.multiple_of((to // 2) * HDIM, HDIM)
                src, dst = (k_ref, v_ref)[kind].at[:, pl.ds(col, HDIM)], own[kind].at[j]
            remote(src, dst, (s, to), y_send.at[kind, to], y_recv.at[kind, j])

    def y_wait(kind):
        here[kind].wait()
        for r in order:
            source = lax.rem(j + ny - r, ny)
            if kind == 3:
                dst = prior.at[:, source]
            else:
                dst = qbuf.at[source] if kind == 2 else own[kind].at[source]
            arrived(dst, y_recv.at[kind, source])

    class Ring:
        def __init__(self, kind, index, slot, n, pos, up, dn, halves, last=1):
            self.sems = (ring_send.at[kind, index], ring_recv.at[kind, index])
            self.slot, self.n, self.pos = slot, n, pos
            self.up, self.dn, self.half, self.halves = up, dn, n // 2, halves
            self.last = last

        def part(self, which, direction, t):
            ref = self.slot(lax.rem(which + self.n, self.n))
            if t < self.half:
                return ref
            if self.halves is not None:
                return ref.at[pl.ds(direction * self.halves, self.halves)]
            return ref if direction == self.last else None

        def start(self, t):
            for direction, sign, to in ((0, -1, self.up), (1, 1, self.dn)):
                part = self.part(self.pos + sign * (t - 1), direction, t)
                if part is not None:
                    sems = [sem.at[direction, t - 1] for sem in self.sems]
                    send(part, to, *sems)

        def wait(self, t):
            for direction, sign in ((0, -1), (1, 1)):
                part = self.part(self.pos + sign * t, direction, t)
                if part is not None:
                    arrived(part, self.sems[1].at[direction, t - 1])

    class Gather:
        def __init__(self, kind):
            self.kind = kind
            self.ax = Ring(
                kind, 0, lambda i: vert.at[kind, 0, core, i], NX, x, up_x, dn_x, NZ // 2
            )
            self.bz = Ring(
                kind, 1, lambda i: vert.at[kind, 1, core, :, i], NZ, z, up_z, dn_z, None, kind
            )
            self.pending = {}

        def row(self, pc, shift):
            return vert.at[self.kind, 0, pc, lax.rem(x + shift + NX, NX)]

        def bundle(self, pc, shift):
            return vert.at[self.kind, 1, pc, :, lax.rem(z + shift + NZ, NZ)]

        def share(self, line, shift):
            n = len(self.pending)
            chunk = self.row if line == 0 else self.bundle
            send(chunk(core, shift), sib, sib_send.at[self.kind, n], sib_recv.at[self.kind, n])
            self.pending[(line, shift)] = n

        def shared(self, line, shift):
            chunk = self.row if line == 0 else self.bundle
            arrived(chunk(1 - core, shift), sib_recv.at[self.kind, self.pending[(line, shift)]])

        def pick(self):
            for m in range(2):
                which = jnp.clip(vert_ref[2 * j + m, s] - s * ny, 0, ny - 1)
                vert[self.kind, m, core, x, z] = own[self.kind][which]

        def line_a(self, n):
            block = lambda i: vert.at[self.kind, 0, core, x, lax.rem(i + NZ, NZ)]
            sems = (az_send.at[self.kind], az_recv.at[self.kind])
            last_x = NX // 2
            sign = 1 if self.kind == 0 else -1
            if n == 0:
                for r in range(reach, 0, -1):
                    for d in (r, -r):
                        send(block(z), along_z[d], sems[0].at[reach + d], sems[1].at[reach + d])
            elif n == 1:
                for r in range(1, reach + 1):
                    for d in (r, -r):
                        arrived(block(z - d), sems[1].at[reach + d])
                to = up_z if sign == 1 else dn_z
                send(block(z - sign * reach), to, sems[0].at[reach], sems[1].at[reach])
            elif n == 2:
                arrived(block(z - sign * (reach + 1)), sems[1].at[reach])
                self.ax.start(1)
                self.share(0, 0)
            else:
                t = n - 2
                if t > last_x:
                    return
                self.ax.wait(t)
                if t < last_x:
                    self.ax.start(t + 1)
                    self.share(0, -t)
                self.share(0, t)

        def line_b(self, n):
            own_chunk = lambda i: vert.at[self.kind, 1, core, lax.rem(i + NX, NX), z]
            sems = (bx_send.at[self.kind], bx_recv.at[self.kind])
            if n == 0:
                for r in range(1, NX):
                    send(own_chunk(x), across_x[r - 1], sems[0].at[r - 1], sems[1].at[r - 1])
            elif n == 1:
                for r in range(1, NX):
                    arrived(own_chunk(x - r), sems[1].at[r - 1])
                self.bz.start(1)
                self.share(1, 0)
            else:
                t = n - 1
                if t > NZ // 2:
                    return
                self.bz.wait(t)
                if t < NZ // 2:
                    self.bz.start(t + 1)
                    self.share(1, -t)
                self.share(1, t)

        def step(self, n):
            self.line_b(n)
            self.line_a(n)

    nt = (((1,), (1,)), ((), ()))
    chunk = ny * BLOCK

    def group(i):
        return slice(i * HDIM, (i + 1) * HDIM)

    def lanes(value, op):
        return functools.reduce(op, [value[:, group(i)] for i in range(value.shape[1] // HDIM)])

    def queries_of(m):
        return qbuf[:, :, m * HDIM : (m + 1) * HDIM].reshape(rows, HDIM)

    def set_near():
        shape = (ny, 2 * chunk)
        place = lax.broadcasted_iota(jnp.int32, shape, 1) // BLOCK
        dist = ny + lax.broadcasted_iota(jnp.int32, shape, 0) - place
        seg_then = jnp.maximum(s - 1, 0)
        least = jnp.where(s > 0, 0, ny)
        for m in range(2):
            head = 2 * j + m
            then = vert_ref[head, seg_then] - seg_then * ny
            now = vert_ref[head, s] - s * ny + ny
            keep = (dist > 0) & ((place == then) | (place == now))
            for i in range(ns):
                keep = keep | (dist == offs_ref[i, head])
            bias_l[m] = jnp.where(keep & (place >= least), 0.0, LOW)

    def near_scores(m, half):
        keys = (prior[0] if half == 0 else own_k[...]).reshape(chunk, HDIM)
        value = lax.dot_general(queries_of(m), keys, nt, preferred_element_type=jnp.float32)
        bias = bias_l[m, :, half * chunk : (half + 1) * chunk]
        value = (value.reshape(ny, BLOCK, chunk) + bias[:, None, :]).reshape(rows, chunk)
        if half == 1:
            line = lax.broadcasted_iota(jnp.int32, (rows, chunk), 0)
            value = jnp.where(
                lax.broadcasted_iota(jnp.int32, (rows, chunk), 1) <= line, value, LOW
            )
        score_l[m, half] = value
        peak[m] = jnp.maximum(peak[m], lanes(value, jnp.maximum))

    def near_values(m, half):
        values = (prior[1] if half == 0 else own_v[...]).reshape(chunk, HDIM)
        top = peak[m]
        parts = [
            jnp.exp2(score_l[m, half, :, group(g)] * RATE - top) for g in range(chunk // HDIM)
        ]
        weight = jnp.concatenate([part.astype(jnp.bfloat16) for part in parts], axis=1)
        sums[m] += functools.reduce(jnp.add, parts)
        acc[m] += jnp.dot(weight, values, preferred_element_type=jnp.float32)

    def far_chunk(m, shift, pc):
        before_here = jnp.maximum((s - pc + NC) // NC - 1, 0)
        if m == 0:
            px = lax.rem(x + shift + NX, NX)
            piece = lax.broadcasted_iota(jnp.int32, (1, NZ * BLOCK), 1) // BLOCK
            return (pc, px), pc * NX + px, px * NZ + piece < before_here, NZ * BLOCK
        pz = lax.rem(z + shift + NZ, NZ)
        piece = lax.broadcasted_iota(jnp.int32, (1, NX * BLOCK), 1) // BLOCK
        where = (pc, slice(None), pz)
        return where, pc * NZ + pz, piece * NZ + pz < before_here, NX * BLOCK

    def far_scores(m, shift):
        store = (score_a, score_b)[m]

        def step(pc, carry):
            where, slot, keep, size = far_chunk(m, shift, pc)
            keys = vert[(0, m) + where].reshape(size, HDIM)
            value = lax.dot_general(queries_of(m), keys, nt, preferred_element_type=jnp.float32)
            value = value + jnp.where(keep, 0.0, LOW)
            store[slot] = value
            peak[m] = jnp.maximum(peak[m], lanes(value, jnp.maximum))
            return carry

        lax.fori_loop(0, NC, step, 0)

    def far_values(m, pc):
        store = (score_a, score_b)[m]

        def step(shift, carry):
            where, slot, _, size = far_chunk(m, shift, pc)
            values = vert[(1, m) + where].reshape(size, HDIM)
            top = peak[m]
            parts = [
                jnp.exp2(store[slot, :, group(g)] * RATE - top) for g in range(size // HDIM)
            ]
            weight = jnp.concatenate([part.astype(jnp.bfloat16) for part in parts], axis=1)
            sums[m] += functools.reduce(jnp.add, parts)
            acc[m] += jnp.dot(weight, values, preferred_element_type=jnp.float32)
            return carry

        lax.fori_loop(0, (NX, NZ)[m], step, 0)

    def set_top(m):
        top = jnp.max(peak[m], axis=1, keepdims=True) * RATE
        peak[m] = jnp.broadcast_to(top, (rows, HDIM))

    stays = []

    def finish(m):
        total = jnp.sum(sums[m], axis=1, keepdims=True)
        obuf[m] = (acc[m] / total).astype(jnp.bfloat16).reshape(ny, BLOCK, HDIM)
        my_col = pl.ds(pl.multiple_of((2 * j + m) * HDIM, HDIM), HDIM)
        for r in order:
            to = lax.rem(j + r, ny)
            remote(
                obuf.at[m, to],
                out_ref.at[:, my_col],
                (s, to),
                out_send.at[m, to],
                out_recv.at[m, j],
            )
        stay = pltpu.make_async_copy(obuf.at[m, j], out_ref.at[:, my_col], misc.at[7 + m])
        stay.start()
        stays.append(stay)

    keys, values = Gather(0), Gather(1)

    def far_shifts(t, n):
        return [0] if t == 0 else [t] if t == n // 2 else [-t, t]

    def scores_of(m, t):
        for shift in far_shifts(t, (NX, NZ)[m]):
            keys.shared(m, shift)
            far_scores(m, shift)

    def values_of(m):
        far_values(m, core)
        for t in range((NX, NZ)[m] // 2 + 1):
            for shift in far_shifts(t, (NX, NZ)[m]):
                values.shared(m, shift)
        far_values(m, 1 - core)

    for kind in range(2):
        remote((k_ref, v_ref)[kind], raw.at[kind], (after, j), misc.at[3 + kind], misc.at[5 + kind])
        y_start(kind)
    peak[...] = jnp.full(peak.shape, LOW, jnp.float32)
    sums[...] = jnp.zeros(sums.shape, jnp.float32)
    acc[...] = jnp.zeros(acc.shape, jnp.float32)
    y_wait(0)
    keys.pick()
    keys.step(0)
    y_wait(1)
    values.pick()
    values.step(0)
    y_start(2)
    for kind in range(2):
        arrived(raw.at[kind], misc.at[5 + kind])
    y_start(3)
    here.append(
        pltpu.make_async_copy(raw.at[:, :, pl.ds(kv_col, HDIM)], prior.at[:, j], misc.at[9])
    )
    here[3].start()
    set_near()

    half_x, half_z = NX // 2, NZ // 2
    steps = max(half_z + 1, half_x + 2)
    work = [
        (3, lambda: y_wait(2)),
        (3, lambda: near_scores(1, 1)),
        (3, lambda: scores_of(1, 0)),
        (3, lambda: near_scores(0, 1)),
    ]
    for t in range(1, half_z + 1):
        work.append((max(4, t + 2), lambda t=t: scores_of(1, t)))
    for t in range(half_x + 1):
        work.append((t + 4, lambda t=t: scores_of(0, t)))
    work.append((steps, lambda: (y_wait(3), near_scores(1, 0), near_scores(0, 0))))
    for n in range(1, steps + 1):
        keys.step(n)
        if n > 1:
            values.step(n - 1)
        for due, unit in work:
            if due == n or (n == steps and due > n):
                unit()
    values.step(steps)
    for m in (1, 0):
        set_top(m)
        near_values(m, 1)
        near_values(m, 0)
        values_of(m)
        finish(m)

    for m in (1, 0):
        for r in order:
            source = lax.rem(j + ny - r, ny)
            col = pl.ds(pl.multiple_of((2 * source + m) * HDIM, HDIM), HDIM)
            arrived(out_ref.at[:, col], out_recv.at[m, source])
    for copy in stays:
        copy.wait()
    for copy in sent:
        copy.wait_send()


def body(queries, keys, values, vertical, offsets):
    ny = lax.axis_size("head")
    ns = offsets.shape[1]
    rows = ny * BLOCK
    nsib = NX + NZ
    half = max(NX, NZ) // 2
    bf16, f32, dma = jnp.bfloat16, jnp.float32, pltpu.SemaphoreType.DMA
    hbm = pl.BlockSpec(memory_space=pltpu.HBM)
    small = pl.BlockSpec(memory_space=pltpu.SMEM)
    segment = pltpu.VMEM((ny, BLOCK, HDIM), bf16)
    return pl.pallas_call(
        functools.partial(kernel, ny, ns),
        out_shape=jax.ShapeDtypeStruct(queries.shape, bf16),
        in_specs=[hbm, hbm, hbm, small, small],
        out_specs=pl.BlockSpec(memory_space=pl.ANY),
        scratch_shapes=[
            pltpu.VMEM((ny, BLOCK, 2 * HDIM), bf16),
            segment,
            segment,
            pltpu.VMEM((2,) + keys.shape, bf16),
            pltpu.VMEM((2, ny, BLOCK, HDIM), bf16),
            pltpu.VMEM((2, 2, NC, NX, NZ, BLOCK, HDIM), bf16),
            pltpu.VMEM((2, ny, 2 * rows), f32),
            pltpu.VMEM((2, 2, rows, rows), f32),
            pltpu.VMEM((NC * NX, rows, NZ * BLOCK), f32),
            pltpu.VMEM((NC * NZ, rows, NX * BLOCK), f32),
            pltpu.VMEM((2, rows, HDIM), f32),
            pltpu.VMEM((2, rows, HDIM), f32),
            pltpu.VMEM((2, rows, HDIM), f32),
            pltpu.VMEM((2, ny, BLOCK, HDIM), bf16),
            dma((4, ny)),
            dma((4, ny)),
            dma((2, 2, 2, half)),
            dma((2, 2, 2, half)),
            dma((2, NX - 1)),
            dma((2, NX - 1)),
            dma((2, NZ - 1)),
            dma((2, NZ - 1)),
            dma((2, nsib)),
            dma((2, nsib)),
            dma((10,)),
            dma((2, ny)),
            dma((2, ny)),
        ],
        compiler_params=pltpu.CompilerParams(
            collective_id=0, has_side_effects=True, vmem_limit_bytes=58 * 1024 * 1024
        ),
    )(queries, keys, values, vertical, offsets.T)


def solution(mesh):
    whole = P(("seq", "head"), None)
    return jax.shard_map(
        body,
        mesh=mesh,
        in_specs=(whole, whole, whole, P(), P()),
        out_specs=whole,
        check_vma=False,
    )
```

```python
import functools
import math

import jax
import jax.numpy as jnp
from jax import lax
from jax.experimental import pallas as pl
from jax.experimental.pallas import tpu as pltpu
from jax.sharding import PartitionSpec as P

HDIM = 128
BLOCK = 64
NX, NZ, NC = 4, 8, 2
LOW = -1e30
RATE = HDIM ** (-0.5) * math.log2(math.e)
MESH = pl.DeviceIdType.MESH


def kernel(
    ny,
    ns,
    q_ref,
    k_ref,
    v_ref,
    vert_ref,
    offs_ref,
    out_ref,
    qbuf,
    own_k,
    own_v,
    raw,
    prior,
    vert,
    bias_l,
    score_l,
    score_a,
    score_b,
    peak,
    sums,
    acc,
    obuf,
    y_send,
    y_recv,
    ring_send,
    ring_recv,
    bx_send,
    bx_recv,
    az_send,
    az_recv,
    sib_send,
    sib_recv,
    misc,
    out_send,
    out_recv,
):
    s = lax.axis_index("seq")
    j = lax.axis_index("head")
    core = lax.rem(s, NC)
    z = lax.rem(s // NC, NZ)
    x = s // (NC * NZ)
    nseq = NX * NZ * NC
    rows = ny * BLOCK
    own = (own_k, own_v)

    def at(px, pz, pc):
        return (lax.rem(px + NX, NX) * NZ + lax.rem(pz + NZ, NZ)) * NC + pc

    up_z, dn_z = at(x, z + 1, core), at(x, z - 1, core)
    up_x, dn_x = at(x + 1, z, core), at(x - 1, z, core)
    sib = at(x, z, 1 - core)
    after = lax.rem(s + 1, nseq)
    before = lax.rem(s + nseq - 1, nseq)
    across_x = [at(x + r, z, core) for r in range(1, NX)]
    reach = NZ // 4
    along_z = {d: at(x, z + d, core) for r in range(1, reach + 1) for d in (r, -r)}
    far_z = {d: other for d, other in along_z.items() if abs(d) > 1}

    kv_col = pl.multiple_of((j // 2) * HDIM, HDIM)
    q_col = pl.multiple_of(j * 2 * HDIM, 2 * HDIM)
    here = [
        pltpu.make_async_copy(k_ref.at[:, pl.ds(kv_col, HDIM)], own_k.at[j], misc.at[0]),
        pltpu.make_async_copy(v_ref.at[:, pl.ds(kv_col, HDIM)], own_v.at[j], misc.at[1]),
        pltpu.make_async_copy(q_ref.at[:, pl.ds(q_col, 2 * HDIM)], qbuf.at[j], misc.at[2]),
    ]
    for copy in here:
        copy.start()

    barrier = pltpu.get_barrier_semaphore()
    for r in range(1, ny):
        pl.semaphore_signal(
            barrier, inc=1, device_id=(s, lax.rem(j + r, ny)), device_id_type=MESH
        )
    others = [up_z, dn_z, sib, after, before] + across_x + list(far_z.values())
    for other in others:
        pl.semaphore_signal(barrier, inc=1, device_id=(other, j), device_id_type=MESH)
    pl.semaphore_wait(barrier, ny - 1 + len(others))

    sent = []

    def remote(src, dst, device, send_sem, recv_sem):
        copy = pltpu.make_async_remote_copy(
            src, dst, send_sem, recv_sem, device_id=device, device_id_type=MESH
        )
        copy.start()
        sent.append(copy)

    def send(src, to, send_sem, recv_sem):
        remote(src, src, (to, j), send_sem, recv_sem)

    def arrived(dst, sem):
        pltpu.make_async_copy(dst, dst, sem).wait()

    order = sorted(range(1, ny), key=lambda r: -min(r, ny - r))

    def y_start(kind):
        for r in order:
            to = lax.rem(j + r, ny)
            if kind == 2:
                col = pl.multiple_of(to * 2 * HDIM, 2 * HDIM)
                src, dst = q_ref.at[:, pl.ds(col, 2 * HDIM)], qbuf.at[j]
            else:
                col = pl.multiple_of((to // 2) * HDIM, HDIM)
                src, dst = (k_ref, v_ref)[kind].at[:, pl.ds(col, HDIM)], own[kind].at[j]
            remote(src, dst, (s, to), y_send.at[kind, to], y_recv.at[kind, j])

    def y_wait(kind):
        here[kind].wait()
        for r in order:
            source = lax.rem(j + ny - r, ny)
            dst = qbuf.at[source] if kind == 2 else own[kind].at[source]
            arrived(dst, y_recv.at[kind, source])

    def to_next(kind):
        return pltpu.make_async_remote_copy(
            (k_ref, v_ref)[kind],
            raw.at[kind],
            misc.at[3 + kind],
            misc.at[5 + kind],
            device_id=(after, j),
            device_id_type=MESH,
        )

    def to_sibling(kind):
        return pltpu.make_async_remote_copy(
            own[kind],
            prior.at[kind],
            misc.at[3 + kind],
            misc.at[5 + kind],
            device_id=(after, j),
            device_id_type=MESH,
        )

    def spread(r):
        to = lax.rem(j + r, ny)
        col = pl.multiple_of((to // 2) * HDIM, HDIM)
        return pltpu.make_async_remote_copy(
            raw.at[:, :, pl.ds(col, HDIM)],
            prior.at[:, j],
            y_send.at[3, to],
            y_recv.at[3, j],
            device_id=(s, to),
            device_id_type=MESH,
        )

    spread_own = pltpu.make_async_copy(
        raw.at[:, :, pl.ds(kv_col, HDIM)], prior.at[:, j], misc.at[9]
    )

    def start_prior(kind, early):
        if early:
            pl.when(core == NC - 1)(lambda: to_next(kind).start())
        else:
            pl.when(core == 0)(lambda: to_sibling(kind).start())

    def spread_prior():
        @pl.when(core == 0)
        def _():
            for kind in range(2):
                arrived(raw.at[kind], misc.at[5 + kind])
            for r in order:
                spread(r).start()
            spread_own.start()

    def take_prior():
        @pl.when(core == 0)
        def _():
            for r in order:
                source = lax.rem(j + ny - r, ny)
                arrived(prior.at[:, source], y_recv.at[3, source])
            spread_own.wait()

        @pl.when(core == NC - 1)
        def _():
            for kind in range(2):
                arrived(prior.at[kind], misc.at[5 + kind])

    def end_prior():
        @pl.when(core == 0)
        def _():
            for kind in range(2):
                to_sibling(kind).wait_send()
            for r in order:
                spread(r).wait_send()

        @pl.when(core == NC - 1)
        def _():
            for kind in range(2):
                to_next(kind).wait_send()

    class Ring:
        def __init__(self, kind, index, slot, n, pos, up, dn, halves, last=1):
            self.sems = (ring_send.at[kind, index], ring_recv.at[kind, index])
            self.slot, self.n, self.pos = slot, n, pos
            self.up, self.dn, self.half, self.halves = up, dn, n // 2, halves
            self.last = last

        def part(self, which, direction, t):
            ref = self.slot(lax.rem(which + self.n, self.n))
            if t < self.half:
                return ref
            if self.halves is not None:
                return ref.at[pl.ds(direction * self.halves, self.halves)]
            return ref if direction == self.last else None

        def start(self, t):
            for direction, sign, to in ((0, -1, self.up), (1, 1, self.dn)):
                part = self.part(self.pos + sign * (t - 1), direction, t)
                if part is not None:
                    sems = [sem.at[direction, t - 1] for sem in self.sems]
                    send(part, to, *sems)

        def wait(self, t):
            for direction, sign in ((0, -1), (1, 1)):
                part = self.part(self.pos + sign * t, direction, t)
                if part is not None:
                    arrived(part, self.sems[1].at[direction, t - 1])

    class Gather:
        def __init__(self, kind):
            self.kind = kind
            self.ax = Ring(
                kind, 0, lambda i: vert.at[kind, 0, core, i], NX, x, up_x, dn_x, NZ // 2
            )
            self.bz = Ring(
                kind, 1, lambda i: vert.at[kind, 1, core, :, i], NZ, z, up_z, dn_z, None, kind
            )
            self.pending = {}

        def row(self, pc, shift):
            return vert.at[self.kind, 0, pc, lax.rem(x + shift + NX, NX)]

        def bundle(self, pc, shift):
            return vert.at[self.kind, 1, pc, :, lax.rem(z + shift + NZ, NZ)]

        def share(self, line, shift):
            n = len(self.pending)
            chunk = self.row if line == 0 else self.bundle
            send(chunk(core, shift), sib, sib_send.at[self.kind, n], sib_recv.at[self.kind, n])
            self.pending[(line, shift)] = n

        def shared(self, line, shift):
            chunk = self.row if line == 0 else self.bundle
            arrived(chunk(1 - core, shift), sib_recv.at[self.kind, self.pending[(line, shift)]])

        def pick(self):
            for m in range(2):
                which = jnp.clip(vert_ref[2 * j + m, s] - s * ny, 0, ny - 1)
                vert[self.kind, m, core, x, z] = own[self.kind][which]

        def line_a(self, n):
            block = lambda i: vert.at[self.kind, 0, core, x, lax.rem(i + NZ, NZ)]
            sems = (az_send.at[self.kind], az_recv.at[self.kind])
            last_x = NX // 2
            side = 1 if self.kind == 0 else -1
            handed = [
                (sign, r)
                for r in range(reach, 0, -1)
                for sign in (1, -1)
                if reach + r < NZ // 2 or sign == side
            ]
            if n == 0:
                for r in range(reach, 0, -1):
                    for d in (r, -r):
                        spot = NZ // 2 + d
                        send(block(z), along_z[d], sems[0].at[spot], sems[1].at[spot])
            elif n == 1:
                for r in range(reach, 0, -1):
                    for d in (r, -r):
                        arrived(block(z - d), sems[1].at[NZ // 2 + d])
                    if r == reach:
                        for sign, r2 in handed:
                            spot = NZ // 2 + sign * (reach + r2)
                            to = along_z[sign * r2]
                            src = block(z - sign * reach)
                            send(src, to, sems[0].at[spot], sems[1].at[spot])
            elif n == 2:
                for sign, r in handed:
                    spot = NZ // 2 + sign * (reach + r)
                    arrived(block(z - sign * (reach + r)), sems[1].at[spot])
                self.ax.start(1)
                self.share(0, 0)
            else:
                t = n - 2
                if t > last_x:
                    return
                self.ax.wait(t)
                if t < last_x:
                    self.ax.start(t + 1)
                    self.share(0, -t)
                self.share(0, t)

        def line_b(self, n):
            own_chunk = lambda i: vert.at[self.kind, 1, core, lax.rem(i + NX, NX), z]
            sems = (bx_send.at[self.kind], bx_recv.at[self.kind])
            if n == 0:
                for r in range(1, NX):
                    send(own_chunk(x), across_x[r - 1], sems[0].at[r - 1], sems[1].at[r - 1])
            elif n == 1:
                for r in range(1, NX):
                    arrived(own_chunk(x - r), sems[1].at[r - 1])
                self.bz.start(1)
                self.share(1, 0)
            else:
                t = n - 1
                if t > NZ // 2:
                    return
                self.bz.wait(t)
                if t < NZ // 2:
                    self.bz.start(t + 1)
                    self.share(1, -t)
                self.share(1, t)

        def step(self, n):
            self.line_b(n)
            self.line_a(n)

    nt = (((1,), (1,)), ((), ()))
    chunk = ny * BLOCK

    def group(i):
        return slice(i * HDIM, (i + 1) * HDIM)

    def lanes(value, op):
        return functools.reduce(op, [value[:, group(i)] for i in range(value.shape[1] // HDIM)])

    def queries_of(m):
        return qbuf[:, :, m * HDIM : (m + 1) * HDIM].reshape(rows, HDIM)

    def set_near():
        shape = (ny, 2 * chunk)
        place = lax.broadcasted_iota(jnp.int32, shape, 1) // BLOCK
        dist = ny + lax.broadcasted_iota(jnp.int32, shape, 0) - place
        seg_then = jnp.maximum(s - 1, 0)
        least = jnp.where(s > 0, 0, ny)
        for m in range(2):
            head = 2 * j + m
            then = vert_ref[head, seg_then] - seg_then * ny
            now = vert_ref[head, s] - s * ny + ny
            keep = (dist > 0) & ((place == then) | (place == now))
            for i in range(ns):
                keep = keep | (dist == offs_ref[i, head])
            bias_l[m] = jnp.where(keep & (place >= least), 0.0, LOW)

    def near_scores(m, half):
        keys = (prior[0] if half == 0 else own_k[...]).reshape(chunk, HDIM)
        value = lax.dot_general(queries_of(m), keys, nt, preferred_element_type=jnp.float32)
        bias = bias_l[m, :, half * chunk : (half + 1) * chunk]
        value = (value.reshape(ny, BLOCK, chunk) + bias[:, None, :]).reshape(rows, chunk)
        if half == 1:
            line = lax.broadcasted_iota(jnp.int32, (rows, chunk), 0)
            value = jnp.where(
                lax.broadcasted_iota(jnp.int32, (rows, chunk), 1) <= line, value, LOW
            )
        score_l[m, half] = value
        peak[m] = jnp.maximum(peak[m], lanes(value, jnp.maximum))

    def add_values(m, part, stored, values):
        top = peak[m, part]
        parts = [
            jnp.exp2(score[part, group(g)] * RATE - top)
            for score in stored
            for g in range(score.shape[1] // HDIM)
        ]
        weight = jnp.concatenate([one.astype(jnp.bfloat16) for one in parts], axis=1)
        sums[m, part] += functools.reduce(jnp.add, parts)
        acc[m, part] += jnp.dot(weight, values, preferred_element_type=jnp.float32)

    def near_values(m, half, part):
        values = (prior[1] if half == 0 else own_v[...]).reshape(chunk, HDIM)
        add_values(m, part, [score_l.at[m, half]], values)

    def far_chunk(m, shift, pc):
        before_here = jnp.maximum((s - pc + NC) // NC - 1, 0)
        if m == 0:
            px = lax.rem(x + shift + NX, NX)
            piece = lax.broadcasted_iota(jnp.int32, (1, NZ * BLOCK), 1) // BLOCK
            return (pc, px), pc * NX + px, px * NZ + piece < before_here, NZ * BLOCK
        pz = lax.rem(z + shift + NZ, NZ)
        piece = lax.broadcasted_iota(jnp.int32, (1, NX * BLOCK), 1) // BLOCK
        where = (pc, slice(None), pz)
        return where, pc * NZ + pz, piece * NZ + pz < before_here, NX * BLOCK

    def far_scores(m, shift):
        store = (score_a, score_b)[m]

        def step(pc, carry):
            where, slot, keep, size = far_chunk(m, shift, pc)
            keys = vert[(0, m) + where].reshape(size, HDIM)
            value = lax.dot_general(queries_of(m), keys, nt, preferred_element_type=jnp.float32)
            value = value + jnp.where(keep, 0.0, LOW)
            store[slot] = value
            peak[m] = jnp.maximum(peak[m], lanes(value, jnp.maximum))
            return carry

        lax.fori_loop(0, NC, step, 0)

    def far_values(m, pc, part):
        both = 1 if m == 0 else 2

        def step(i, carry):
            found = [far_chunk(m, i * both + k, pc) for k in range(both)]
            values = [vert[(1, m) + where].reshape(size, HDIM) for where, _, _, size in found]
            stored = [(score_a, score_b)[m].at[slot] for _, slot, _, _ in found]
            add_values(m, part, stored, jnp.concatenate(values, axis=0))
            return carry

        lax.fori_loop(0, (NX, NZ)[m] // both, step, 0)

    def set_top(m):
        top = jnp.max(peak[m], axis=1, keepdims=True) * RATE
        peak[m] = jnp.broadcast_to(top, (rows, HDIM))


    def finish(m, first, count):
        part = slice(first * BLOCK, (first + count) * BLOCK)
        total = jnp.sum(sums[m, part], axis=1, keepdims=True)
        result = (acc[m, part] / total).astype(jnp.bfloat16)
        obuf[m, first : first + count] = result.reshape(count, BLOCK, HDIM)
        my_col = pl.ds(pl.multiple_of((2 * j + m) * HDIM, HDIM), HDIM)
        for to in range(first, first + count):

            @pl.when(to != j)
            def _():
                out_copy(m, to, my_col).start()

            @pl.when(to == j)
            def _():
                stay_copy(m, to, my_col).start()

    def out_copy(m, to, my_col):
        return pltpu.make_async_remote_copy(
            obuf.at[m, to],
            out_ref.at[:, my_col],
            out_send.at[m, to],
            out_recv.at[m, j],
            device_id=(s, to),
            device_id_type=MESH,
        )

    def stay_copy(m, to, my_col):
        return pltpu.make_async_copy(obuf.at[m, to], out_ref.at[:, my_col], misc.at[7 + m])

    keys, values = Gather(0), Gather(1)

    def far_shifts(t, n):
        return [0] if t == 0 else [t] if t == n // 2 else [-t, t]

    def scores_of(m, t):
        for shift in far_shifts(t, (NX, NZ)[m]):
            keys.shared(m, shift)
            far_scores(m, shift)

    def take_shared(m):
        for t in range((NX, NZ)[m] // 2 + 1):
            for shift in far_shifts(t, (NX, NZ)[m]):
                values.shared(m, shift)

    for kind in range(2):
        start_prior(kind, True)
        y_start(kind)
    peak[...] = jnp.full(peak.shape, LOW, jnp.float32)
    sums[...] = jnp.zeros(sums.shape, jnp.float32)
    acc[...] = jnp.zeros(acc.shape, jnp.float32)
    y_wait(0)
    keys.pick()
    keys.step(0)
    y_wait(1)
    values.pick()
    values.step(0)
    y_start(2)
    for kind in range(2):
        start_prior(kind, False)
    set_near()

    half_x, half_z = NX // 2, NZ // 2
    steps = max(half_z + 1, half_x + 2)
    work = {
        3: [lambda: y_wait(2), lambda: near_scores(1, 1), lambda: near_scores(0, 1)],
        4: [lambda: scores_of(1, 0), lambda: scores_of(1, 1)],
    }
    for n in range(1, steps):
        keys.step(n)
        if n > 1:
            values.step(n - 1)
        else:
            spread_prior()
        if n in work:
            for unit in work.pop(n):
                unit()
    values.step(steps - 1)
    for n in sorted(work):
        for unit in work[n]:
            unit()
    for t in range(half_x):
        scores_of(0, t)
    keys.step(steps)
    scores_of(0, half_x)
    take_prior()
    near_scores(0, 0)
    near_scores(1, 0)
    every = slice(0, rows)
    set_top(0)
    near_values(0, 1, every)
    near_values(0, 0, every)
    values.step(steps)
    far_values(0, core, every)
    take_shared(0)
    far_values(0, 1 - core, every)
    finish(0, 0, ny)
    for t in range(2, half_z + 1):
        scores_of(1, t)
    set_top(1)
    take_shared(1)
    count = ny // 2
    for first in (0, count):
        part = slice(first * BLOCK, (first + count) * BLOCK)
        near_values(1, 1, part)
        near_values(1, 0, part)
        for pc in range(NC):
            far_values(1, pc, part)
        finish(1, first, count)

    for m in range(2):
        my_col = pl.ds(pl.multiple_of((2 * j + m) * HDIM, HDIM), HDIM)
        for r in order:
            source = lax.rem(j + ny - r, ny)
            col = pl.ds(pl.multiple_of((2 * source + m) * HDIM, HDIM), HDIM)
            arrived(out_ref.at[:, col], out_recv.at[m, source])
            out_copy(m, lax.rem(j + r, ny), my_col).wait_send()
        stay_copy(m, j, my_col).wait()
    end_prior()
    for copy in sent:
        copy.wait_send()


def body(queries, keys, values, vertical, offsets):
    ny = lax.axis_size("head")
    ns = offsets.shape[1]
    rows = ny * BLOCK
    nsib = NX + NZ
    half = max(NX, NZ) // 2
    bf16, f32, dma = jnp.bfloat16, jnp.float32, pltpu.SemaphoreType.DMA
    hbm = pl.BlockSpec(memory_space=pltpu.HBM)
    small = pl.BlockSpec(memory_space=pltpu.SMEM)
    segment = pltpu.VMEM((ny, BLOCK, HDIM), bf16)
    return pl.pallas_call(
        functools.partial(kernel, ny, ns),
        out_shape=jax.ShapeDtypeStruct(queries.shape, bf16),
        in_specs=[hbm, hbm, hbm, small, small],
        out_specs=pl.BlockSpec(memory_space=pl.ANY),
        scratch_shapes=[
            pltpu.VMEM((ny, BLOCK, 2 * HDIM), bf16),
            segment,
            segment,
            pltpu.VMEM((2,) + keys.shape, bf16),
            pltpu.VMEM((2, ny, BLOCK, HDIM), bf16),
            pltpu.VMEM((2, 2, NC, NX, NZ, BLOCK, HDIM), bf16),
            pltpu.VMEM((2, ny, 2 * rows), f32),
            pltpu.VMEM((2, 2, rows, rows), f32),
            pltpu.VMEM((NC * NX, rows, NZ * BLOCK), f32),
            pltpu.VMEM((NC * NZ, rows, NX * BLOCK), f32),
            pltpu.VMEM((2, rows, HDIM), f32),
            pltpu.VMEM((2, rows, HDIM), f32),
            pltpu.VMEM((2, rows, HDIM), f32),
            pltpu.VMEM((2, ny, BLOCK, HDIM), bf16),
            dma((4, ny)),
            dma((4, ny)),
            dma((2, 2, 2, half)),
            dma((2, 2, 2, half)),
            dma((2, NX - 1)),
            dma((2, NX - 1)),
            dma((2, NZ + 1)),
            dma((2, NZ + 1)),
            dma((2, nsib)),
            dma((2, nsib)),
            dma((10,)),
            dma((2, ny)),
            dma((2, ny)),
        ],
        compiler_params=pltpu.CompilerParams(
            collective_id=0, has_side_effects=True, vmem_limit_bytes=58 * 1024 * 1024
        ),
    )(queries, keys, values, vertical, offsets.T)


def solution(mesh):
    whole = P(("seq", "head"), None)
    return jax.shard_map(
        body,
        mesh=mesh,
        in_specs=(whole, whole, whole, P(), P()),
        out_specs=whole,
        check_vma=False,
    )
```

```python
import functools
import math

import jax
import jax.numpy as jnp
from jax import lax
from jax.experimental import pallas as pl
from jax.experimental.pallas import tpu as pltpu
from jax.sharding import PartitionSpec as P

HDIM = 128
BLOCK = 64
NX, NZ, NC = 4, 8, 2
LOW = -1e30
RATE = HDIM ** (-0.5) * math.log2(math.e)
MESH = pl.DeviceIdType.MESH


def kernel(
    ny,
    ns,
    q_ref,
    k_ref,
    v_ref,
    vert_ref,
    offs_ref,
    out_ref,
    qbuf,
    own_k,
    own_v,
    raw,
    prior,
    vert,
    bias_l,
    score_l,
    score_a,
    score_b,
    peak,
    sums,
    acc,
    obuf,
    y_send,
    y_recv,
    ring_send,
    ring_recv,
    bx_send,
    bx_recv,
    az_send,
    az_recv,
    sib_send,
    sib_recv,
    misc,
    out_send,
    out_recv,
):
    s = lax.axis_index("seq")
    j = lax.axis_index("head")
    core = lax.rem(s, NC)
    z = lax.rem(s // NC, NZ)
    x = s // (NC * NZ)
    nseq = NX * NZ * NC
    rows = ny * BLOCK
    own = (own_k, own_v)

    def at(px, pz, pc):
        return (lax.rem(px + NX, NX) * NZ + lax.rem(pz + NZ, NZ)) * NC + pc

    up_z, dn_z = at(x, z + 1, core), at(x, z - 1, core)
    up_x, dn_x = at(x + 1, z, core), at(x - 1, z, core)
    sib = at(x, z, 1 - core)
    after = lax.rem(s + 1, nseq)
    before = lax.rem(s + nseq - 1, nseq)
    across_x = [at(x + r, z, core) for r in range(1, NX)]
    reach = NZ // 4
    along_z = {d: at(x, z + d, core) for r in range(1, reach + 1) for d in (r, -r)}
    far_z = {d: other for d, other in along_z.items() if abs(d) > 1}

    kv_col = pl.multiple_of((j // 2) * HDIM, HDIM)
    q_col = pl.multiple_of(j * 2 * HDIM, 2 * HDIM)
    here = [
        pltpu.make_async_copy(k_ref.at[:, pl.ds(kv_col, HDIM)], own_k.at[j], misc.at[0]),
        pltpu.make_async_copy(v_ref.at[:, pl.ds(kv_col, HDIM)], own_v.at[j], misc.at[1]),
        pltpu.make_async_copy(q_ref.at[:, pl.ds(q_col, 2 * HDIM)], qbuf.at[j], misc.at[2]),
    ]
    for copy in here:
        copy.start()

    barrier = pltpu.get_barrier_semaphore()
    for r in range(1, ny):
        pl.semaphore_signal(
            barrier, inc=1, device_id=(s, lax.rem(j + r, ny)), device_id_type=MESH
        )
    others = [up_z, dn_z, sib, after, before] + across_x + list(far_z.values())
    for other in others:
        pl.semaphore_signal(barrier, inc=1, device_id=(other, j), device_id_type=MESH)
    pl.semaphore_wait(barrier, ny - 1 + len(others))

    sent = []

    def remote(src, dst, device, send_sem, recv_sem):
        copy = pltpu.make_async_remote_copy(
            src, dst, send_sem, recv_sem, device_id=device, device_id_type=MESH
        )
        copy.start()
        sent.append(copy)

    def send(src, to, send_sem, recv_sem):
        remote(src, src, (to, j), send_sem, recv_sem)

    def arrived(dst, sem):
        pltpu.make_async_copy(dst, dst, sem).wait()

    order = sorted(range(1, ny), key=lambda r: -min(r, ny - r))

    def y_start(kind):
        for r in order:
            to = lax.rem(j + r, ny)
            if kind == 2:
                col = pl.multiple_of(to * 2 * HDIM, 2 * HDIM)
                src, dst = q_ref.at[:, pl.ds(col, 2 * HDIM)], qbuf.at[j]
            else:
                col = pl.multiple_of((to // 2) * HDIM, HDIM)
                src, dst = (k_ref, v_ref)[kind].at[:, pl.ds(col, HDIM)], own[kind].at[j]
            remote(src, dst, (s, to), y_send.at[kind, to], y_recv.at[kind, j])

    def y_wait(kind):
        here[kind].wait()
        for r in order:
            source = lax.rem(j + ny - r, ny)
            dst = qbuf.at[source] if kind == 2 else own[kind].at[source]
            arrived(dst, y_recv.at[kind, source])

    def to_next(kind):
        return pltpu.make_async_remote_copy(
            (k_ref, v_ref)[kind],
            raw.at[kind],
            misc.at[3 + kind],
            misc.at[5 + kind],
            device_id=(after, j),
            device_id_type=MESH,
        )

    def to_sibling(kind):
        return pltpu.make_async_remote_copy(
            own[kind],
            prior.at[kind],
            misc.at[3 + kind],
            misc.at[5 + kind],
            device_id=(after, j),
            device_id_type=MESH,
        )

    def spread(r):
        to = lax.rem(j + r, ny)
        col = pl.multiple_of((to // 2) * HDIM, HDIM)
        return pltpu.make_async_remote_copy(
            raw.at[:, :, pl.ds(col, HDIM)],
            prior.at[:, j],
            y_send.at[3, to],
            y_recv.at[3, j],
            device_id=(s, to),
            device_id_type=MESH,
        )

    spread_own = pltpu.make_async_copy(
        raw.at[:, :, pl.ds(kv_col, HDIM)], prior.at[:, j], misc.at[9]
    )

    def start_prior(kind, early):
        if early:
            pl.when(core == NC - 1)(lambda: to_next(kind).start())
        else:
            pl.when(core == 0)(lambda: to_sibling(kind).start())

    def spread_prior():
        @pl.when(core == 0)
        def _():
            for kind in range(2):
                arrived(raw.at[kind], misc.at[5 + kind])
            for r in order:
                spread(r).start()
            spread_own.start()

    def take_prior():
        @pl.when(core == 0)
        def _():
            for r in order:
                source = lax.rem(j + ny - r, ny)
                arrived(prior.at[:, source], y_recv.at[3, source])
            spread_own.wait()

        @pl.when(core == NC - 1)
        def _():
            for kind in range(2):
                arrived(prior.at[kind], misc.at[5 + kind])

    def end_prior():
        @pl.when(core == 0)
        def _():
            for kind in range(2):
                to_sibling(kind).wait_send()
            for r in order:
                spread(r).wait_send()

        @pl.when(core == NC - 1)
        def _():
            for kind in range(2):
                to_next(kind).wait_send()

    class Ring:
        def __init__(self, kind, index, slot, n, pos, up, dn, halves, last=1):
            self.sems = (ring_send.at[kind, index], ring_recv.at[kind, index])
            self.slot, self.n, self.pos = slot, n, pos
            self.up, self.dn, self.half, self.halves = up, dn, n // 2, halves
            self.last = last

        def part(self, which, direction, t):
            ref = self.slot(lax.rem(which + self.n, self.n))
            if t < self.half:
                return ref
            if self.halves is not None:
                return ref.at[pl.ds(direction * self.halves, self.halves)]
            return ref if direction == self.last else None

        def start(self, t):
            for direction, sign, to in ((0, -1, self.up), (1, 1, self.dn)):
                part = self.part(self.pos + sign * (t - 1), direction, t)
                if part is not None:
                    sems = [sem.at[direction, t - 1] for sem in self.sems]
                    send(part, to, *sems)

        def wait(self, t):
            for direction, sign in ((0, -1), (1, 1)):
                part = self.part(self.pos + sign * t, direction, t)
                if part is not None:
                    arrived(part, self.sems[1].at[direction, t - 1])

    class Gather:
        def __init__(self, kind):
            self.kind = kind
            self.ax = Ring(
                kind, 0, lambda i: vert.at[kind, 0, core, i], NX, x, up_x, dn_x, NZ // 2
            )
            self.bz = Ring(
                kind, 1, lambda i: vert.at[kind, 1, core, :, i], NZ, z, up_z, dn_z, None, kind
            )
            self.pending = {}

        def row(self, pc, shift):
            return vert.at[self.kind, 0, pc, lax.rem(x + shift + NX, NX)]

        def bundle(self, pc, shift):
            return vert.at[self.kind, 1, pc, :, lax.rem(z + shift + NZ, NZ)]

        def share(self, line, shift):
            n = len(self.pending)
            chunk = self.row if line == 0 else self.bundle
            send(chunk(core, shift), sib, sib_send.at[self.kind, n], sib_recv.at[self.kind, n])
            self.pending[(line, shift)] = n

        def shared(self, line, shift):
            chunk = self.row if line == 0 else self.bundle
            arrived(chunk(1 - core, shift), sib_recv.at[self.kind, self.pending[(line, shift)]])

        def pick(self):
            for m in range(2):
                which = jnp.clip(vert_ref[2 * j + m, s] - s * ny, 0, ny - 1)
                vert[self.kind, m, core, x, z] = own[self.kind][which]

        def line_a(self, n):
            block = lambda i: vert.at[self.kind, 0, core, x, lax.rem(i + NZ, NZ)]
            sems = (az_send.at[self.kind], az_recv.at[self.kind])
            last_x = NX // 2
            side = 1 if self.kind == 0 else -1
            handed = [
                (sign, r)
                for r in range(reach, 0, -1)
                for sign in (1, -1)
                if reach + r < NZ // 2 or sign == side
            ]
            if n == 0:
                for r in range(reach, 0, -1):
                    for d in (r, -r):
                        spot = NZ // 2 + d
                        send(block(z), along_z[d], sems[0].at[spot], sems[1].at[spot])
            elif n == 1:
                for r in range(reach, 0, -1):
                    for d in (r, -r):
                        arrived(block(z - d), sems[1].at[NZ // 2 + d])
                    if r == reach:
                        for sign, r2 in handed:
                            spot = NZ // 2 + sign * (reach + r2)
                            to = along_z[sign * r2]
                            src = block(z - sign * reach)
                            send(src, to, sems[0].at[spot], sems[1].at[spot])
            elif n == 2:
                for sign, r in handed:
                    spot = NZ // 2 + sign * (reach + r)
                    arrived(block(z - sign * (reach + r)), sems[1].at[spot])
                self.ax.start(1)
                self.share(0, 0)
            else:
                t = n - 2
                if t > last_x:
                    return
                self.ax.wait(t)
                if t < last_x:
                    self.ax.start(t + 1)
                    self.share(0, -t)
                self.share(0, t)

        def line_b(self, n):
            own_chunk = lambda i: vert.at[self.kind, 1, core, lax.rem(i + NX, NX), z]
            sems = (bx_send.at[self.kind], bx_recv.at[self.kind])
            if n == 0:
                for r in range(1, NX):
                    send(own_chunk(x), across_x[r - 1], sems[0].at[r - 1], sems[1].at[r - 1])
            elif n == 1:
                for r in range(1, NX):
                    arrived(own_chunk(x - r), sems[1].at[r - 1])
                self.bz.start(1)
                self.share(1, 0)
            else:
                t = n - 1
                if t > NZ // 2:
                    return
                self.bz.wait(t)
                if t < NZ // 2:
                    self.bz.start(t + 1)
                    self.share(1, -t)
                self.share(1, t)

        def step(self, n):
            self.line_b(n)
            self.line_a(n)

    nt = (((1,), (1,)), ((), ()))
    chunk = ny * BLOCK

    def group(i):
        return slice(i * HDIM, (i + 1) * HDIM)

    def lanes(value, op):
        return functools.reduce(op, [value[:, group(i)] for i in range(value.shape[1] // HDIM)])

    def queries_of(m):
        return qbuf[:, :, m * HDIM : (m + 1) * HDIM].reshape(rows, HDIM)

    def set_near():
        shape = (ny, 2 * chunk)
        place = lax.broadcasted_iota(jnp.int32, shape, 1) // BLOCK
        dist = ny + lax.broadcasted_iota(jnp.int32, shape, 0) - place
        seg_then = jnp.maximum(s - 1, 0)
        least = jnp.where(s > 0, 0, ny)
        for m in range(2):
            head = 2 * j + m
            then = vert_ref[head, seg_then] - seg_then * ny
            now = vert_ref[head, s] - s * ny + ny
            keep = (dist > 0) & ((place == then) | (place == now))
            for i in range(ns):
                keep = keep | (dist == offs_ref[i, head])
            bias_l[m] = jnp.where(keep & (place >= least), 0.0, LOW)

    def near_scores(m, half, late=False):
        keys = (prior[0] if half == 0 else own_k[...]).reshape(chunk, HDIM)
        value = lax.dot_general(queries_of(m), keys, nt, preferred_element_type=jnp.float32)
        bias = bias_l[m, :, half * chunk : (half + 1) * chunk]
        value = (value.reshape(ny, BLOCK, chunk) + bias[:, None, :]).reshape(rows, chunk)
        if half == 1:
            line = lax.broadcasted_iota(jnp.int32, (rows, chunk), 0)
            value = jnp.where(
                lax.broadcasted_iota(jnp.int32, (rows, chunk), 1) <= line, value, LOW
            )
        score_l[m, half] = value
        best = lanes(value, jnp.maximum)
        if late:
            top = peak[m]
            raised = jnp.maximum(top, jnp.max(best, axis=1, keepdims=True) * RATE)
            factor = jnp.exp2(top - raised)
            peak[m] = raised
            sums[m] *= factor
            acc[m] *= factor
        else:
            peak[m] = jnp.maximum(peak[m], best)

    def add_values(m, part, stored, values):
        top = peak[m, part]
        parts = [
            jnp.exp2(score[part, group(g)] * RATE - top)
            for score in stored
            for g in range(score.shape[1] // HDIM)
        ]
        weight = jnp.concatenate([one.astype(jnp.bfloat16) for one in parts], axis=1)
        sums[m, part] += functools.reduce(jnp.add, parts)
        acc[m, part] += jnp.dot(weight, values, preferred_element_type=jnp.float32)

    def near_values(m, half, part):
        values = (prior[1] if half == 0 else own_v[...]).reshape(chunk, HDIM)
        add_values(m, part, [score_l.at[m, half]], values)

    def far_chunk(m, shift, pc):
        before_here = jnp.maximum((s - pc + NC) // NC - 1, 0)
        if m == 0:
            px = lax.rem(x + shift + NX, NX)
            piece = lax.broadcasted_iota(jnp.int32, (1, NZ * BLOCK), 1) // BLOCK
            return (pc, px), pc * NX + px, px * NZ + piece < before_here, NZ * BLOCK
        pz = lax.rem(z + shift + NZ, NZ)
        piece = lax.broadcasted_iota(jnp.int32, (1, NX * BLOCK), 1) // BLOCK
        where = (pc, slice(None), pz)
        return where, pc * NZ + pz, piece * NZ + pz < before_here, NX * BLOCK

    def far_scores(m, shift):
        store = (score_a, score_b)[m]

        def step(pc, carry):
            where, slot, keep, size = far_chunk(m, shift, pc)
            keys = vert[(0, m) + where].reshape(size, HDIM)
            value = lax.dot_general(queries_of(m), keys, nt, preferred_element_type=jnp.float32)
            value = value + jnp.where(keep, 0.0, LOW)
            store[slot] = value
            peak[m] = jnp.maximum(peak[m], lanes(value, jnp.maximum))
            return carry

        lax.fori_loop(0, NC, step, 0)

    def far_values(m, pc, part):
        both = 1 if m == 0 else 2

        def step(i, carry):
            found = [far_chunk(m, i * both + k, pc) for k in range(both)]
            values = [vert[(1, m) + where].reshape(size, HDIM) for where, _, _, size in found]
            stored = [(score_a, score_b)[m].at[slot] for _, slot, _, _ in found]
            add_values(m, part, stored, jnp.concatenate(values, axis=0))
            return carry

        lax.fori_loop(0, (NX, NZ)[m] // both, step, 0)

    def set_top(m):
        top = jnp.max(peak[m], axis=1, keepdims=True) * RATE
        peak[m] = jnp.broadcast_to(top, (rows, HDIM))


    def finish(m, first, count):
        part = slice(first * BLOCK, (first + count) * BLOCK)
        total = jnp.sum(sums[m, part], axis=1, keepdims=True)
        result = (acc[m, part] / total).astype(jnp.bfloat16)
        obuf[m, first : first + count] = result.reshape(count, BLOCK, HDIM)
        my_col = pl.ds(pl.multiple_of((2 * j + m) * HDIM, HDIM), HDIM)
        for to in range(first, first + count):

            @pl.when(to != j)
            def _():
                out_copy(m, to, my_col).start()

            @pl.when(to == j)
            def _():
                stay_copy(m, to, my_col).start()

    def out_copy(m, to, my_col):
        return pltpu.make_async_remote_copy(
            obuf.at[m, to],
            out_ref.at[:, my_col],
            out_send.at[m, to],
            out_recv.at[m, j],
            device_id=(s, to),
            device_id_type=MESH,
        )

    def stay_copy(m, to, my_col):
        return pltpu.make_async_copy(obuf.at[m, to], out_ref.at[:, my_col], misc.at[7 + m])

    keys, values = Gather(0), Gather(1)

    def far_shifts(t, n):
        return [0] if t == 0 else [t] if t == n // 2 else [-t, t]

    def scores_of(m, t):
        for shift in far_shifts(t, (NX, NZ)[m]):
            keys.shared(m, shift)
            far_scores(m, shift)

    def take_shared(m):
        for t in range((NX, NZ)[m] // 2 + 1):
            for shift in far_shifts(t, (NX, NZ)[m]):
                values.shared(m, shift)

    for kind in range(2):
        start_prior(kind, True)
        y_start(kind)
    peak[...] = jnp.full(peak.shape, LOW, jnp.float32)
    sums[...] = jnp.zeros(sums.shape, jnp.float32)
    acc[...] = jnp.zeros(acc.shape, jnp.float32)
    y_wait(0)
    keys.pick()
    keys.step(0)
    y_wait(1)
    values.pick()
    values.step(0)
    y_start(2)
    for kind in range(2):
        start_prior(kind, False)
    set_near()

    half_x, half_z = NX // 2, NZ // 2
    steps = max(half_z + 1, half_x + 2)
    work = {
        3: [lambda: y_wait(2), lambda: near_scores(1, 1), lambda: near_scores(0, 1)],
        4: [lambda: scores_of(1, 0), lambda: scores_of(1, 1)],
    }
    for n in range(1, steps):
        keys.step(n)
        if n > 1:
            values.step(n - 1)
        else:
            spread_prior()
        if n in work:
            for unit in work.pop(n):
                unit()
    values.step(steps - 1)
    for n in sorted(work):
        for unit in work[n]:
            unit()
    for t in range(half_x):
        scores_of(0, t)
    keys.step(steps)
    scores_of(0, half_x)
    every = slice(0, rows)
    set_top(0)
    near_values(0, 1, every)
    far_values(0, core, every)
    values.step(steps)
    take_shared(0)
    far_values(0, 1 - core, every)
    for t in range(2, half_z + 1):
        scores_of(1, t)
    take_prior()
    near_scores(0, 0, late=True)
    near_values(0, 0, every)
    finish(0, 0, ny)
    near_scores(1, 0)
    set_top(1)
    take_shared(1)
    count = ny // 2
    for first in (0, count):
        part = slice(first * BLOCK, (first + count) * BLOCK)
        near_values(1, 1, part)
        near_values(1, 0, part)
        for pc in range(NC):
            far_values(1, pc, part)
        finish(1, first, count)

    for m in range(2):
        my_col = pl.ds(pl.multiple_of((2 * j + m) * HDIM, HDIM), HDIM)
        for r in order:
            source = lax.rem(j + ny - r, ny)
            col = pl.ds(pl.multiple_of((2 * source + m) * HDIM, HDIM), HDIM)
            arrived(out_ref.at[:, col], out_recv.at[m, source])
            out_copy(m, lax.rem(j + r, ny), my_col).wait_send()
        stay_copy(m, j, my_col).wait()
    end_prior()
    for copy in sent:
        copy.wait_send()


def body(queries, keys, values, vertical, offsets):
    ny = lax.axis_size("head")
    ns = offsets.shape[1]
    rows = ny * BLOCK
    nsib = NX + NZ
    half = max(NX, NZ) // 2
    bf16, f32, dma = jnp.bfloat16, jnp.float32, pltpu.SemaphoreType.DMA
    hbm = pl.BlockSpec(memory_space=pltpu.HBM)
    small = pl.BlockSpec(memory_space=pltpu.SMEM)
    segment = pltpu.VMEM((ny, BLOCK, HDIM), bf16)
    return pl.pallas_call(
        functools.partial(kernel, ny, ns),
        out_shape=jax.ShapeDtypeStruct(queries.shape, bf16),
        in_specs=[hbm, hbm, hbm, small, small],
        out_specs=pl.BlockSpec(memory_space=pl.ANY),
        scratch_shapes=[
            pltpu.VMEM((ny, BLOCK, 2 * HDIM), bf16),
            segment,
            segment,
            pltpu.VMEM((2,) + keys.shape, bf16),
            pltpu.VMEM((2, ny, BLOCK, HDIM), bf16),
            pltpu.VMEM((2, 2, NC, NX, NZ, BLOCK, HDIM), bf16),
            pltpu.VMEM((2, ny, 2 * rows), f32),
            pltpu.VMEM((2, 2, rows, rows), f32),
            pltpu.VMEM((NC * NX, rows, NZ * BLOCK), f32),
            pltpu.VMEM((NC * NZ, rows, NX * BLOCK), f32),
            pltpu.VMEM((2, rows, HDIM), f32),
            pltpu.VMEM((2, rows, HDIM), f32),
            pltpu.VMEM((2, rows, HDIM), f32),
            pltpu.VMEM((2, ny, BLOCK, HDIM), bf16),
            dma((4, ny)),
            dma((4, ny)),
            dma((2, 2, 2, half)),
            dma((2, 2, 2, half)),
            dma((2, NX - 1)),
            dma((2, NX - 1)),
            dma((2, NZ + 1)),
            dma((2, NZ + 1)),
            dma((2, nsib)),
            dma((2, nsib)),
            dma((10,)),
            dma((2, ny)),
            dma((2, ny)),
        ],
        compiler_params=pltpu.CompilerParams(
            collective_id=0, has_side_effects=True, vmem_limit_bytes=58 * 1024 * 1024
        ),
    )(queries, keys, values, vertical, offsets.T)


def solution(mesh):
    whole = P(("seq", "head"), None)
    return jax.shard_map(
        body,
        mesh=mesh,
        in_specs=(whole, whole, whole, P(), P()),
        out_specs=whole,
        check_vma=False,
    )
```
